32 devices in a mesh: dp: 16 (over z, y, core), seq: 2 (over x).
Axes of the slice: x: 2, y: 2, z: 4, core: 2. Of those that a mesh axis runs over, the one named last changes fastest.
Arguments:
- tokens: bfloat16 [256, 4096], P('seq', 'dp'), may hold values from -6 to 6
- in_weight: bfloat16 [2, 4096, 8192], P(None, 'seq', 'dp'), may hold values from -0.09375 to 0.09375
- conv_weight: bfloat16 [4, 8192], P(None, 'dp'), may hold values from -0.5 to 0.5
- conv_bias: bfloat16 [8192], P('dp'), may hold values from -1 to 1
- out_weight: bfloat16 [8192, 4096], P('dp', 'seq'), may hold values from -0.0625 to 0.0625
- grad_out: bfloat16 [256, 4096], P('seq', 'dp'), may hold values from -6 to 6
Outputs:
- output: bfloat16 [256, 4096], P('seq', 'dp')
- grad_tokens: bfloat16 [256, 4096], P('seq', 'dp')
- grad_in_weight: float32 [2, 4096, 8192], P(None, 'seq', 'dp')
- grad_out_weight: float32 [8192, 4096], P('dp', 'seq')
- grad_conv_weight: float32 [4, 8192], P(None, 'dp')
- grad_conv_bias: float32 [8192], P('dp')
The draws below stay inside these ranges and needn't reach their ends.
All inputs are finite; a program needn't handle non-finite values.
Results may differ from the reference program's by a relative error of at most 0.012.
Values may be sent and summed in bfloat16 or wider, within the bound.
A program may use at most 128 MiB of HBM per device.

```python
import jax
import jax.numpy as jnp
from jax import lax

D = 4096
E = 8192
KERNEL = 4
TOK_DEV = 128
TOKENS = 256
N_SEQ = 2


def block_scale(rng, shape, cuts, low, top_value):
    def one(axis_at, parts):
        heights = jax.random.uniform(jax.random.fold_in(jax.random.fold_in(rng, 6), axis_at), (parts,), jnp.float32, low / len(cuts), top_value / len(cuts))
        return jnp.repeat(jnp.exp(heights), shape[axis_at] // parts).reshape((-1,) + (1,) * (len(shape) - axis_at - 1))

    level = one(*cuts[0])
    for cut in cuts[1:]:
        level = level * one(*cut)
    return level


def centred(own_key, extent, deviation, bound, shards=(), kind=jnp.bfloat16):
    result = jax.random.normal(own_key, extent, jnp.float32) * deviation
    if len(shards) > 0:
        result = block_scale(own_key, extent, shards, -0.22, 0.18) * result
    return jnp.clip(result, min=-bound, max=bound).astype(kind)


def setup_inputs(seed: int = 0) -> dict:
    keys = jax.random.split(jax.random.key(seed), 7)
    tokens = centred(keys[0], (TOKENS, D), 1.0, 6.0, ((0, 2), (1, 16)))
    in_weight = centred(keys[1], (2, D, E), D ** -0.5, 0.09375, ((1, 2), (2, 16)))
    conv_weight = jnp.clip(jax.random.uniform(keys[2], (KERNEL, E), jnp.float32, -0.5, 0.5) * block_scale(keys[2], (KERNEL, E), ((1, 16),), -0.4, 0.0), -0.5, 0.5).astype(jnp.bfloat16)
    conv_bias = jnp.clip(jax.random.uniform(keys[3], (E,), jnp.float32, -1.0, 1.0) * block_scale(keys[3], (E,), ((0, 16),), -0.4, 0.0), -1.0, 1.0).astype(jnp.bfloat16)
    out_weight = centred(keys[4], (E, D), E ** -0.5, 0.0625, ((0, 16), (1, 2)))
    grad_out = centred(keys[5], (TOKENS, D), 1.0, 6.0, ((0, 2), (1, 16)))
    return {"tokens": tokens, "in_weight": in_weight, "conv_weight": conv_weight, "conv_bias": conv_bias, "out_weight": out_weight, "grad_out": grad_out}


def silu_parts(value):
    sig = jax.nn.sigmoid(value)
    return value * sig, sig * (1.0 + value * (1.0 - sig))


def reference(tokens, in_weight, conv_weight, conv_bias, out_weight, grad_out):
    inner = jnp.dot(tokens, in_weight[0], preferred_element_type=jnp.float32).astype(jnp.bfloat16)
    gate_in = jnp.dot(tokens, in_weight[1], preferred_element_type=jnp.float32).astype(jnp.bfloat16)
    padded = jnp.concatenate([jnp.zeros((KERNEL - 1, E), jnp.bfloat16), inner], axis=0)
    conv = jnp.broadcast_to(conv_bias.astype(jnp.float32)[None, :], (TOKENS, E))
    for lag in range(KERNEL):
        conv = conv + conv_weight[lag].astype(jnp.float32)[None, :] * padded[lag:lag + TOKENS].astype(jnp.float32)
    act, act_slope = silu_parts(conv)
    gate, gate_slope = silu_parts(gate_in.astype(jnp.float32))
    hidden = (act * gate).astype(jnp.bfloat16)
    output = jnp.dot(hidden, out_weight, preferred_element_type=jnp.float32).astype(jnp.bfloat16)
    back = lax.dot_general(grad_out, out_weight, (((1,), (1,)), ((), ())), preferred_element_type=jnp.float32)
    grad_conv = (back * gate * act_slope).astype(jnp.bfloat16)
    grad_gate = (back * act * gate_slope).astype(jnp.bfloat16)
    ahead = jnp.concatenate([grad_conv, jnp.zeros((KERNEL - 1, E), jnp.bfloat16)], axis=0)
    grad_inner = jnp.zeros((TOKENS, E), jnp.float32)
    for lag in range(KERNEL):
        shift_start = KERNEL - 1 - lag
        grad_inner = grad_inner + conv_weight[lag].astype(jnp.float32)[None, :] * ahead[shift_start:shift_start + TOKENS].astype(jnp.float32)
    grad_inner = grad_inner.astype(jnp.bfloat16)
    grad_tokens = lax.dot_general(grad_inner, in_weight[0], (((1,), (1,)), ((), ())), preferred_element_type=jnp.float32)
    grad_tokens = grad_tokens + lax.dot_general(grad_gate, in_weight[1], (((1,), (1,)), ((), ())), preferred_element_type=jnp.float32)
    grad_tokens = grad_tokens.astype(jnp.bfloat16)
    conv_float = grad_conv.astype(jnp.float32)
    tap_rows = []
    for lag in range(KERNEL):
        tap_rows.append(jnp.sum(conv_float * padded[lag:lag + TOKENS].astype(jnp.float32), axis=0))
    grad_conv_weight = jnp.stack(tap_rows, axis=0)
    grad_conv_bias = jnp.sum(conv_float, axis=0)

    def accumulate(block, carry):
        sum_in, sum_out = carry
        first = (block * TOK_DEV).astype(jnp.int32)
        rows = lax.dynamic_slice_in_dim(tokens, first, TOK_DEV, 0)
        inner_rows = lax.dynamic_slice_in_dim(grad_inner, first, TOK_DEV, 0)
        gate_rows = lax.dynamic_slice_in_dim(grad_gate, first, TOK_DEV, 0)
        hidden_rows = lax.dynamic_slice_in_dim(hidden, first, TOK_DEV, 0)
        upstream_rows = lax.dynamic_slice_in_dim(grad_out, first, TOK_DEV, 0)
        term_inner = lax.dot_general(rows, inner_rows, (((0,), (0,)), ((), ())), preferred_element_type=jnp.float32)
        term_gate = lax.dot_general(rows, gate_rows, (((0,), (0,)), ((), ())), preferred_element_type=jnp.float32)
        term_in = jnp.stack([term_inner, term_gate], axis=0).astype(jnp.bfloat16).astype(jnp.float32)
        term_out = lax.dot_general(hidden_rows, upstream_rows, (((0,), (0,)), ((), ())), preferred_element_type=jnp.float32)
        term_out = term_out.astype(jnp.bfloat16).astype(jnp.float32)
        return sum_in + term_in, sum_out + term_out

    start_carry = (jnp.zeros((2, D, E), jnp.float32), jnp.zeros((E, D), jnp.float32))
    grad_in_weight, grad_out_weight = lax.fori_loop(0, N_SEQ, accumulate, start_carry)
    return output, grad_tokens, grad_in_weight, grad_out_weight, grad_conv_weight, grad_conv_bias
```

```python
import jax
import jax.numpy as jnp
from jax import lax
from jax.sharding import PartitionSpec as P


def silu_parts(value):
    sig = jax.nn.sigmoid(value)
    return (value * sig, sig * (1.0 + value * (1.0 - sig)))


def routes():
    n, m = lax.axis_size("dp"), lax.axis_size("seq")
    per = n // m
    there = [
        (j * m + t, (t * per + j % per) * m + j // per) for j in range(n) for t in range(m)
    ]
    return there, [(b, a) for a, b in there]


def on_device(tokens, in_weight, conv_weight, conv_bias, out_weight, grad_out):
    n, m = lax.axis_size("dp"), lax.axis_size("seq")
    per = n // m
    rows, cols = tokens.shape
    total = rows * m
    width = per * cols
    taps, chans = conv_weight.shape
    there, back_route = routes()

    both = jnp.stack([tokens, grad_out])
    moved = lax.ppermute(both, ("dp", "seq"), there)
    gathered = lax.all_gather(moved, "dp")
    arranged = gathered.reshape(m, per, 2, rows, cols).transpose(2, 0, 3, 1, 4)
    arranged = arranged.reshape(2, total, width)
    whole, upstream = arranged[0], arranged[1]

    mixed = jnp.einsum("td,pde->pte", whole, in_weight, preferred_element_type=jnp.float32)
    back_part = lax.dot_general(
        upstream, out_weight, (((1,), (1,)), ((), ())), preferred_element_type=jnp.float32
    )
    parts = jnp.concatenate(
        [mixed.astype(jnp.bfloat16), back_part.astype(jnp.bfloat16)[None]], axis=0
    )
    parts = lax.all_gather(parts, "seq").astype(jnp.float32)
    sums = parts[0]
    for i in range(1, m):
        sums = sums + parts[i]
    inner = sums[0].astype(jnp.bfloat16).astype(jnp.float32)
    gate_in = sums[1].astype(jnp.bfloat16).astype(jnp.float32)
    back = sums[2]

    zeros = jnp.zeros((taps - 1, chans), jnp.float32)
    padded = jnp.concatenate([zeros, inner], axis=0)
    taps_f = conv_weight.astype(jnp.float32)
    conv = jnp.broadcast_to(conv_bias.astype(jnp.float32)[None, :], inner.shape)
    for lag in range(taps):
        conv = conv + taps_f[lag][None, :] * padded[lag : lag + total]
    act, act_slope = silu_parts(conv)
    gate, gate_slope = silu_parts(gate_in)
    hidden = (act * gate).astype(jnp.bfloat16)
    grad_conv = (back * gate * act_slope).astype(jnp.bfloat16).astype(jnp.float32)
    grad_gate = (back * act * gate_slope).astype(jnp.bfloat16)
    ahead = jnp.concatenate([grad_conv, zeros], axis=0)
    grad_inner = jnp.zeros(inner.shape, jnp.float32)
    for lag in range(taps):
        start = taps - 1 - lag
        grad_inner = grad_inner + taps_f[lag][None, :] * ahead[start : start + total]
    grad_inner = grad_inner.astype(jnp.bfloat16)
    tap_grads = jnp.stack(
        [jnp.sum(grad_conv * padded[lag : lag + total], axis=0) for lag in range(taps)], axis=0
    )
    bias_grads = jnp.sum(grad_conv, axis=0)

    out_part = jnp.dot(hidden, out_weight, preferred_element_type=jnp.float32)
    contract = (((1,), (1,)), ((), ()))
    tok_part = lax.dot_general(
        grad_inner, in_weight[0], contract, preferred_element_type=jnp.float32
    ) + lax.dot_general(grad_gate, in_weight[1], contract, preferred_element_type=jnp.float32)
    sent = jnp.stack([out_part.astype(jnp.bfloat16), tok_part.astype(jnp.bfloat16)])
    sent = sent.reshape(2, m, rows, per, cols).transpose(1, 3, 0, 2, 4)
    sent = sent.reshape(n, 2, rows, cols)
    summed = lax.psum_scatter(sent, "dp", scatter_dimension=0, tiled=False)
    result = lax.ppermute(summed, ("dp", "seq"), back_route)

    branch = jnp.stack([grad_inner, grad_gate])
    grad_in_weight = jnp.einsum(
        "td,pte->pde", whole, branch, preferred_element_type=jnp.float32
    )
    grad_out_weight = lax.dot_general(
        hidden, upstream, (((0,), (0,)), ((), ())), preferred_element_type=jnp.float32
    )
    return (result[0], result[1], grad_in_weight, grad_out_weight, tap_grads, bias_grads)


def solution(mesh):
    return jax.shard_map(
        on_device,
        mesh=mesh,
        in_specs=(
            P("seq", "dp"),
            P(None, "seq", "dp"),
            P(None, "dp"),
            P("dp"),
            P("dp", "seq"),
            P("seq", "dp"),
        ),
        out_specs=(
            P("seq", "dp"),
            P("seq", "dp"),
            P(None, "seq", "dp"),
            P("dp", "seq"),
            P(None, "dp"),
            P("dp"),
        ),
        check_vma=False,
    )
```

```python
import functools

import jax
import jax.numpy as jnp
from jax import lax
from jax.experimental import pallas as pl
from jax.experimental.pallas import tpu as pltpu
from jax.sharding import PartitionSpec as P

F32, BF16 = jnp.float32, jnp.bfloat16
MESH = pl.DeviceIdType.MESH
NT = (((1,), (1,)), ((), ()))
TN = (((0,), (0,)), ((), ()))


def silu_parts(value):
    sig = jax.nn.sigmoid(value)
    return (value * sig, sig * (1.0 + value * (1.0 - sig)))


def split_dp(n):
    pairs = n // 2
    ys = 2 ** ((pairs.bit_length() - 1) // 2)
    return pairs // ys, ys


def body(
    n, m, tok, gout, win_hbm, cw_ref, cb_ref, wout_hbm,
    out_ref, gtok_ref, x_ref, g_ref, hid_ref, gi_ref, gg_ref, tap_ref, bias_ref,
    win, wout, pack, gat, slot, part, rcore, ry, rz, fin, res, pad, pad2,
    w_sem, sw_send, sw_recv, gz_send, gy_send, gc_send, g_recv, ex_send, ex_recv,
    rc_send, rc_recv, ry_send, ry_recv, rz_send, rz_recv,
):
    zs, ys = split_dp(n)
    per = n // m
    rows, cols = tok.shape
    total = rows * m
    taps, chans = cw_ref.shape
    chunks, width = slot.shape[1], slot.shape[4]
    dp, seq = lax.axis_index("dp"), lax.axis_index("seq")
    z, y, c = dp // (2 * ys), (dp // 2) % ys, dp % 2
    other = 1 - c

    def at(zz, yy, cc):
        return (zz * ys + yy) * 2 + cc

    mate = {"dp": seq * per + dp % per, "seq": dp // per}
    swaps = dp // per != seq

    def send(src, dst, ssem, rsem, where):
        return pltpu.make_async_remote_copy(
            src_ref=src, dst_ref=dst, send_sem=ssem, recv_sem=rsem,
            device_id=where, device_id_type=MESH,
        )

    loads = [
        pltpu.make_async_copy(win_hbm, win, w_sem.at[0]),
        pltpu.make_async_copy(wout_hbm, wout, w_sem.at[1]),
    ]
    for load in loads:
        load.start()

    barrier = pltpu.get_barrier_semaphore()
    near = [{"dp": at(z, y, other)}]
    near += [{"dp": at(z, (y + d) % ys, c)} for d in range(1, ys)]
    near += [{"dp": at((z + d) % zs, y, c)} for d in range(1, zs)]
    near += [{"seq": (seq + d) % m} for d in range(1, m)]
    for where in near:
        pl.semaphore_signal(barrier, inc=1, device_id=where, device_id_type=MESH)

    @pl.when(swaps)
    def _():
        pl.semaphore_signal(barrier, inc=1, device_id=mate, device_id_type=MESH)

    pl.semaphore_wait(barrier, len(near) + swaps.astype(jnp.int32))

    @pl.when(swaps)
    def _():
        pack[0] = tok[...]
        pack[1] = gout[...]
        copy = send(pack, gat.at[mate["dp"]], sw_send.at[0], sw_recv.at[0], mate)
        copy.start()
        copy.wait_send()
        send(pack, gat.at[dp], sw_send.at[0], sw_recv.at[0], mate).wait_recv()

    @pl.when(jnp.logical_not(swaps))
    def _():
        gat[dp, 0] = tok[...]
        gat[dp, 1] = gout[...]

    def arrived(q):
        send(gat.at[q], gat.at[q], gc_send.at[0], g_recv.at[q], mate).wait_recv()

    sent = []

    def forward(q, ssem, where):
        copy = send(gat.at[q], gat.at[q], ssem, g_recv.at[q], where)
        copy.start()
        sent.append(copy)

    for d in range(1, zs):
        forward(dp, gz_send.at[d - 1], {"dp": at((z + d) % zs, y, c)})
    for d in range(zs):
        q = at((z + d) % zs, y, c)
        if d:
            arrived(q)
        for e in range(1, ys):
            forward(q, gy_send.at[d * (ys - 1) + e - 1], {"dp": at(z, (y + e) % ys, c)})
        forward(q, gc_send.at[d * ys], {"dp": at(z, y, other)})
    for d in range(zs):
        for e in range(1, ys):
            q = at((z + d) % zs, (y + e) % ys, c)
            arrived(q)
            forward(q, gc_send.at[d * ys + e], {"dp": at(z, y, other)})
    for d in range(zs):
        for e in range(ys):
            arrived(at((z + d) % zs, (y + e) % ys, other))
    for q in range(n):
        t, j = q // per, q % per
        x_ref[t * rows : (t + 1) * rows, j * cols : (j + 1) * cols] = gat[q, 0]
        g_ref[t * rows : (t + 1) * rows, j * cols : (j + 1) * cols] = gat[q, 1]
    for load in loads:
        load.wait()

    for k in range(chunks):
        span = slice(k * width, (k + 1) * width)
        for p in range(2):
            slot[seq, k, p] = jnp.dot(
                x_ref[...], win[p, :, span], preferred_element_type=F32
            ).astype(BF16)
        slot[seq, k, 2] = lax.dot_general(
            g_ref[...], wout[span, :], NT, preferred_element_type=F32
        ).astype(BF16)
        for d in range(1, m):
            copy = send(
                slot.at[seq, k], slot.at[seq, k], ex_send.at[k * (m - 1) + d - 1],
                ex_recv.at[k * m + seq], {"seq": (seq + d) % m},
            )
            copy.start()
            sent.append(copy)

    pad[0:8] = jnp.zeros((8, pad.shape[1]), F32)
    pad2[total : total + 8] = jnp.zeros((8, pad.shape[1]), F32)
    lanes = pad.shape[1]
    taps_f = cw_ref[...].astype(F32)
    shift_f = cb_ref[...].astype(F32)
    for k in range(chunks):
        for d in range(1, m):
            peer = (seq + d) % m
            send(
                slot.at[peer, k], slot.at[peer, k], ex_send.at[0],
                ex_recv.at[k * m + peer], mate,
            ).wait_recv()
        for col in range(0, width, lanes):
            local = slice(col, col + lanes)
            span = slice(k * width + col, k * width + col + lanes)

            def summed(p):
                value = slot[0, k, p, :, local].astype(F32)
                for i in range(1, m):
                    value = value + slot[i, k, p, :, local].astype(F32)
                return value

            pad[8 : 8 + total] = summed(0).astype(BF16).astype(F32)
            gate, gate_slope = silu_parts(summed(1).astype(BF16).astype(F32))
            conv = jnp.broadcast_to(shift_f[:, span], (total, lanes))
            for lag in range(taps):
                first = 9 - taps + lag
                conv = conv + taps_f[lag : lag + 1, span] * pad[first : first + total]
            act, act_slope = silu_parts(conv)
            back = summed(2)
            hid_ref[:, span] = (act * gate).astype(BF16)
            gg_ref[:, span] = (back * act * gate_slope).astype(BF16)
            grad_conv = (back * gate * act_slope).astype(BF16).astype(F32)
            pad2[0:total] = grad_conv
            grad_inner = jnp.zeros((total, lanes), F32)
            for lag in range(taps):
                first = taps - 1 - lag
                grad_inner = grad_inner + taps_f[lag : lag + 1, span] * pad2[first : first + total]
            gi_ref[:, span] = grad_inner.astype(BF16)
            for lag in range(taps):
                first = 9 - taps + lag
                tap_ref[lag : lag + 1, span] = jnp.sum(
                    grad_conv * pad[first : first + total], axis=0, keepdims=True
                )
            bias_ref[:, span] = jnp.sum(grad_conv, axis=0, keepdims=True)

    for j in range(per):
        span = slice(j * cols, (j + 1) * cols)
        first = jnp.dot(hid_ref[...], wout[:, span], preferred_element_type=F32)
        second = lax.dot_general(gi_ref[...], win[0, span, :], NT, preferred_element_type=F32)
        second = second + lax.dot_general(
            gg_ref[...], win[1, span, :], NT, preferred_element_type=F32
        )
        for t in range(m):
            part[t * per + j, 0] = first[t * rows : (t + 1) * rows].astype(BF16)
            part[t * per + j, 1] = second[t * rows : (t + 1) * rows].astype(BF16)

    order = [(d, e) for e in range(ys - 1, -1, -1) for d in range(zs - 1, -1, -1)]

    def core_copy(d, e, which):
        zz, yy = (z + d) % zs, (y + e) % ys
        i = zz * ys + yy
        return send(part.at[at(zz, yy, which)], rcore.at[i], rc_send.at[i], rc_recv.at[i],
                    {"dp": at(z, y, other)})

    for d, e in order:
        copy = core_copy(d, e, other)
        copy.start()
        sent.append(copy)
    for e in range(ys - 1, 0, -1):
        for d in range(zs - 1, -1, -1):
            zz, yy = (z + d) % zs, (y + e) % ys
            core_copy(d, e, other).wait_recv()
            q = at(zz, yy, c)
            part[q] = (part[q].astype(F32) + rcore[zz * ys + yy].astype(F32)).astype(BF16)
            i = (e - 1) * zs + zz
            copy = send(part.at[q], ry.at[i], ry_send.at[i], ry_recv.at[i], {"dp": at(z, yy, c)})
            copy.start()
            sent.append(copy)
    for d in range(zs - 1, -1, -1):
        zz = (z + d) % zs
        core_copy(d, 0, other).wait_recv()
        q = at(zz, y, c)
        value = part[q].astype(F32) + rcore[zz * ys + y].astype(F32)
        for e in range(1, ys):
            i = (e - 1) * zs + zz
            send(part.at[q], ry.at[i], ry_send.at[i], ry_recv.at[i], mate).wait_recv()
            value = value + ry[i].astype(F32)
        if d:
            part[q] = value.astype(BF16)
            copy = send(part.at[q], rz.at[d - 1], rz_send.at[d - 1], rz_recv.at[d - 1],
                        {"dp": at(zz, y, c)})
            copy.start()
            sent.append(copy)
        else:
            for i in range(zs - 1):
                send(part.at[q], rz.at[i], rz_send.at[i], rz_recv.at[i], mate).wait_recv()
                value = value + rz[i].astype(F32)
            fin[...] = value.astype(BF16)

    @pl.when(swaps)
    def _():
        copy = send(fin, res, sw_send.at[1], sw_recv.at[1], mate)
        copy.start()
        copy.wait()
        out_ref[...] = res[0]
        gtok_ref[...] = res[1]

    @pl.when(jnp.logical_not(swaps))
    def _():
        out_ref[...] = fin[0]
        gtok_ref[...] = fin[1]

    for copy in sent:
        copy.wait_send()


def weight_grads(x_ref, g_ref, hid_ref, gi_ref, gg_ref, din_ref, dout_ref):
    x = x_ref[...]
    din_ref[0] = lax.dot_general(x, gi_ref[...], TN, preferred_element_type=F32)
    din_ref[1] = lax.dot_general(x, gg_ref[...], TN, preferred_element_type=F32)
    dout_ref[...] = lax.dot_general(hid_ref[...], g_ref[...], TN, preferred_element_type=F32)


def on_device(tokens, in_weight, conv_weight, conv_bias, out_weight, grad_out):
    n, m = lax.axis_size("dp"), lax.axis_size("seq")
    zs, ys = split_dp(n)
    rows, cols = tokens.shape
    total = rows * m
    depth = in_weight.shape[1]
    taps, chans = conv_weight.shape
    width = min(chans, 256)
    chunks = chans // width
    lanes = min(width, 128)
    vmem = pl.BlockSpec(memory_space=pltpu.VMEM)
    hbm = pl.BlockSpec(memory_space=pl.ANY)
    dma = lambda count: pltpu.SemaphoreType.DMA((max(count, 1),))
    pair = (2, rows, cols)
    shape = jax.ShapeDtypeStruct
    flops = 2 * total * depth * chans * 6
    out, gtok, x, g, hid, gi, gg, tap, bias = pl.pallas_call(
        functools.partial(body, n, m),
        out_shape=(
            shape((rows, cols), BF16), shape((rows, cols), BF16),
            shape((total, depth), BF16), shape((total, depth), BF16),
            shape((total, chans), BF16), shape((total, chans), BF16),
            shape((total, chans), BF16),
            shape((taps, chans), F32), shape((1, chans), F32),
        ),
        in_specs=[vmem, vmem, hbm, vmem, vmem, hbm],
        out_specs=(vmem,) * 9,
        scratch_shapes=[
            pltpu.VMEM(in_weight.shape, BF16),
            pltpu.VMEM(out_weight.shape, BF16),
            pltpu.VMEM(pair, BF16),
            pltpu.VMEM((n,) + pair, BF16),
            pltpu.VMEM((m, chunks, 3, total, width), BF16),
            pltpu.VMEM((n,) + pair, BF16),
            pltpu.VMEM((zs * ys,) + pair, BF16),
            pltpu.VMEM((max(zs * (ys - 1), 1),) + pair, BF16),
            pltpu.VMEM((max(zs - 1, 1),) + pair, BF16),
            pltpu.VMEM(pair, BF16),
            pltpu.VMEM(pair, BF16),
            pltpu.VMEM((total + 8, lanes), F32),
            pltpu.VMEM((total + 8, lanes), F32),
            dma(2), dma(2), dma(2),
            dma(zs - 1), dma(zs * (ys - 1)), dma(zs * ys), dma(n),
            dma(chunks * (m - 1)), dma(chunks * m),
            dma(zs * ys), dma(zs * ys),
            dma(zs * (ys - 1)), dma(zs * (ys - 1)),
            dma(zs - 1), dma(zs - 1),
        ],
        compiler_params=pltpu.CompilerParams(
            collective_id=0, has_side_effects=True, vmem_limit_bytes=56 * 2**20
        ),
        cost_estimate=pl.CostEstimate(
            flops=flops, bytes_accessed=12 * 2**20, transcendentals=2 * total * chans
        ),
        name="mixer",
    )(tokens, grad_out, in_weight, conv_weight, conv_bias.reshape(1, chans), out_weight)

    tile = min(depth, 256)
    whole = pl.BlockSpec((total, chans), lambda i: (0, 0))
    strip = pl.BlockSpec((total, tile), lambda i: (0, i))
    din, dout = pl.pallas_call(
        weight_grads,
        grid=(depth // tile,),
        out_shape=(shape(in_weight.shape, F32), shape(out_weight.shape, F32)),
        in_specs=[strip, strip, whole, whole, whole],
        out_specs=(
            pl.BlockSpec((2, tile, chans), lambda i: (0, i, 0)),
            pl.BlockSpec((chans, tile), lambda i: (0, i)),
        ),
        compiler_params=pltpu.CompilerParams(vmem_limit_bytes=32 * 2**20),
        name="weight_grads",
    )(x, g, hid, gi, gg)
    return (out, gtok, din, dout, tap, bias.reshape(chans))


def solution(mesh):
    return jax.shard_map(
        on_device,
        mesh=mesh,
        in_specs=(
            P("seq", "dp"),
            P(None, "seq", "dp"),
            P(None, "dp"),
            P("dp"),
            P("dp", "seq"),
            P("seq", "dp"),
        ),
        out_specs=(
            P("seq", "dp"),
            P("seq", "dp"),
            P(None, "seq", "dp"),
            P("dp", "seq"),
            P(None, "dp"),
            P("dp"),
        ),
        check_vma=False,
    )
```

```python
import functools

import jax
import jax.numpy as jnp
from jax import lax
from jax.experimental import pallas as pl
from jax.experimental.pallas import tpu as pltpu
from jax.sharding import PartitionSpec as P

F32, BF16 = jnp.float32, jnp.bfloat16
MESH = pl.DeviceIdType.MESH
NT = (((1,), (1,)), ((), ()))
TN = (((0,), (0,)), ((), ()))


def silu_parts(value):
    sig = jax.nn.sigmoid(value)
    return (value * sig, sig * (1.0 + value * (1.0 - sig)))


def split_dp(n):
    pairs = n // 2
    ys = 2 ** ((pairs.bit_length() - 1) // 2)
    return pairs // ys, ys


def body(
    n, m, tok, gout, win_hbm, cw_ref, cb_ref, wout_hbm,
    out_ref, gtok_ref, x_ref, g_ref, hid_ref, gi_ref, gg_ref, tap_ref, bias_ref,
    win, wout, gat, slot, bslot, part, rcore, ry, rz, fin, res, pad, pad2, sa, sb,
    w_sem, sw_send, sw_recv, gz_send, gy_send, gc_send, g_recv, ex_send, ex_recv,
    bx_send, bx_recv, rc_send, rc_recv, ry_send, ry_recv, rz_send, rz_recv,
):
    zs, ys = split_dp(n)
    per = n // m
    rows, cols = tok.shape
    total = rows * m
    taps, chans = cw_ref.shape
    chunks, width = slot.shape[1], slot.shape[4]
    lanes = pad2.shape[1]
    dp, seq = lax.axis_index("dp"), lax.axis_index("seq")
    z, y, c = dp // (2 * ys), (dp // 2) % ys, dp % 2
    other = 1 - c

    def at(zz, yy, cc):
        return (zz * ys + yy) * 2 + cc

    mate = {"dp": seq * per + dp % per, "seq": dp // per}
    swaps = dp // per != seq

    def send(src, dst, ssem, rsem, where):
        return pltpu.make_async_remote_copy(
            src_ref=src, dst_ref=dst, send_sem=ssem, recv_sem=rsem,
            device_id=where, device_id_type=MESH,
        )

    loads = [
        pltpu.make_async_copy(win_hbm, win, w_sem.at[0]),
        pltpu.make_async_copy(wout_hbm, wout, w_sem.at[1]),
    ]
    for load in loads:
        load.start()

    barrier = pltpu.get_barrier_semaphore()
    near = [{"dp": at(z, y, other)}]
    near += [{"dp": at(z, (y + d) % ys, c)} for d in range(1, ys)]
    near += [{"dp": at((z + d) % zs, y, c)} for d in range(1, zs)]
    near += [{"seq": (seq + d) % m} for d in range(1, m)]
    for where in near:
        pl.semaphore_signal(barrier, inc=1, device_id=where, device_id_type=MESH)

    @pl.when(swaps)
    def _():
        pl.semaphore_signal(barrier, inc=1, device_id=mate, device_id_type=MESH)

    pl.semaphore_wait(barrier, len(near) + swaps.astype(jnp.int32))

    sent = []

    def go(*args):
        copy = send(*args)
        copy.start()
        sent.append(copy)

    def gathered(p, q, ssem, where):
        go(gat.at[p, q], gat.at[p, q], ssem, g_recv.at[p, q], where)

    def arrived(p, q):
        here = gat.at[p, q]
        send(here, here, gc_send.at[p, 0], g_recv.at[p, q], mate).wait_recv()

    sources = (tok, gout)

    def swap_in(p):
        return send(sources[p], gat.at[p, mate["dp"]], sw_send.at[p], sw_recv.at[p], mate)

    @pl.when(swaps)
    def _():
        for p in range(2):
            swap_in(p).start()
        for p in range(2):
            swap_in(p).wait_send()

    def own_block(p):
        @pl.when(swaps)
        def _():
            send(gat.at[p, dp], gat.at[p, dp], sw_send.at[p], sw_recv.at[p], mate).wait_recv()

        @pl.when(jnp.logical_not(swaps))
        def _():
            gat[p, dp] = sources[p][...]

        for d in range(1, zs):
            gathered(p, dp, gz_send.at[p, d - 1], {"dp": at((z + d) % zs, y, c)})

    def along_z(p):
        for d in range(zs):
            q = at((z + d) % zs, y, c)
            if d:
                arrived(p, q)
            for e in range(1, ys):
                i = d * (ys - 1) + e - 1
                gathered(p, q, gy_send.at[p, i], {"dp": at(z, (y + e) % ys, c)})
            gathered(p, q, gc_send.at[p, d * ys], {"dp": at(z, y, other)})

    def along_y(p, dest):
        for d in range(zs):
            for e in range(1, ys):
                q = at((z + d) % zs, (y + e) % ys, c)
                arrived(p, q)
                gathered(p, q, gc_send.at[p, d * ys + e], {"dp": at(z, y, other)})
        for d in range(zs):
            for e in range(ys):
                arrived(p, at((z + d) % zs, (y + e) % ys, other))
        for q in range(n):
            t, j = q // per, q % per
            dest[t * rows : (t + 1) * rows, j * cols : (j + 1) * cols] = gat[p, q]

    own_block(0)
    along_z(0)
    own_block(1)
    along_y(0, x_ref)
    for load in loads:
        load.wait()

    for k in range(chunks):
        span = slice(k * width, (k + 1) * width)
        for p in range(2):
            slot[seq, k, p] = jnp.dot(
                x_ref[...], win[p, :, span], preferred_element_type=F32
            ).astype(BF16)
        for d in range(1, m):
            here = slot.at[seq, k]
            go(here, here, ex_send.at[k * (m - 1) + d - 1], ex_recv.at[k * m + seq],
               {"seq": (seq + d) % m})
    along_z(1)
    along_y(1, g_ref)
    for k in range(chunks):
        span = slice(k * width, (k + 1) * width)
        bslot[seq, :, span] = lax.dot_general(
            g_ref[...], wout[span, :], NT, preferred_element_type=F32
        ).astype(BF16)
    for d in range(1, m):
        here = bslot.at[seq]
        go(here, here, bx_send.at[d - 1], bx_recv.at[seq], {"seq": (seq + d) % m})

    def over_seq(read):
        value = read(0).astype(F32)
        for i in range(1, m):
            value = value + read(i).astype(F32)
        return value

    pad[0:8] = jnp.zeros((8, chans), F32)
    pad2[total : total + 8] = jnp.zeros((8, lanes), F32)
    taps_f = cw_ref[...].astype(F32)
    shift_f = cb_ref[...].astype(F32)
    for k in range(chunks):
        for d in range(1, m):
            peer = (seq + d) % m
            here = slot.at[peer, k]
            send(here, here, ex_send.at[0], ex_recv.at[k * m + peer], mate).wait_recv()
        for col in range(0, width, lanes):
            local = slice(col, col + lanes)
            span = slice(k * width + col, k * width + col + lanes)
            inner = over_seq(lambda i: slot[i, k, 0, :, local])
            pad[8 : 8 + total, span] = inner.astype(BF16).astype(F32)
            gate_in = over_seq(lambda i: slot[i, k, 1, :, local])
            gate, gate_slope = silu_parts(gate_in.astype(BF16).astype(F32))
            conv = jnp.broadcast_to(shift_f[:, span], (total, lanes))
            for lag in range(taps):
                first = 9 - taps + lag
                conv = conv + taps_f[lag : lag + 1, span] * pad[first : first + total, span]
            act, act_slope = silu_parts(conv)
            hid_ref[:, span] = (act * gate).astype(BF16)
            sa[:, span] = gate * act_slope
            sb[:, span] = act * gate_slope

    def core_copy(p, d, e, which):
        zz, yy = (z + d) % zs, (y + e) % ys
        i = zz * ys + yy
        return send(part.at[p, at(zz, yy, which)], rcore.at[p, i], rc_send.at[p, i],
                    rc_recv.at[p, i], {"dp": at(z, y, other)})

    def to_core(p):
        for e in range(ys - 1, -1, -1):
            for d in range(zs - 1, -1, -1):
                copy = core_copy(p, d, e, other)
                copy.start()
                sent.append(copy)

    def to_y(p):
        for e in range(ys - 1, 0, -1):
            for d in range(zs - 1, -1, -1):
                zz, yy = (z + d) % zs, (y + e) % ys
                core_copy(p, d, e, other).wait_recv()
                q = at(zz, yy, c)
                value = part[p, q].astype(F32) + rcore[p, zz * ys + yy].astype(F32)
                part[p, q] = value.astype(BF16)
                i = (e - 1) * zs + zz
                go(part.at[p, q], ry.at[p, i], ry_send.at[p, i], ry_recv.at[p, i],
                   {"dp": at(z, yy, c)})

    def to_z(p):
        for d in range(zs - 1, -1, -1):
            zz = (z + d) % zs
            core_copy(p, d, 0, other).wait_recv()
            q = at(zz, y, c)
            value = part[p, q].astype(F32) + rcore[p, zz * ys + y].astype(F32)
            for e in range(1, ys):
                i = (e - 1) * zs + zz
                send(part.at[p, q], ry.at[p, i], ry_send.at[p, i], ry_recv.at[p, i],
                     mate).wait_recv()
                value = value + ry[p, i].astype(F32)
            if d:
                part[p, q] = value.astype(BF16)
                go(part.at[p, q], rz.at[p, d - 1], rz_send.at[p, d - 1], rz_recv.at[p, d - 1],
                   {"dp": at(zz, y, c)})
            else:
                part[p, q] = value.astype(BF16)

    def swap_out(p):
        return send(fin.at[p], res.at[p], sw_send.at[2 + p], sw_recv.at[2 + p], mate)

    def finish(p):
        value = part[p, dp].astype(F32)
        for i in range(zs - 1):
            send(part.at[p, dp], rz.at[p, i], rz_send.at[p, i], rz_recv.at[p, i],
                 mate).wait_recv()
            value = value + rz[p, i].astype(F32)
        fin[p] = value.astype(BF16)

        @pl.when(swaps)
        def _():
            swap_out(p).start()

    for j in range(per):
        span = slice(j * cols, (j + 1) * cols)
        value = jnp.dot(hid_ref[...], wout[:, span], preferred_element_type=F32)
        for t in range(m):
            part[0, t * per + j] = value[t * rows : (t + 1) * rows].astype(BF16)
    to_core(0)
    to_y(0)

    for d in range(1, m):
        here = bslot.at[(seq + d) % m]
        send(here, here, bx_send.at[0], bx_recv.at[(seq + d) % m], mate).wait_recv()
    for col in range(0, chans, lanes):
        span = slice(col, col + lanes)
        back = over_seq(lambda i: bslot[i, :, span])
        gg_ref[:, span] = (back * sb[:, span]).astype(BF16)
        grad_conv = (back * sa[:, span]).astype(BF16).astype(F32)
        pad2[0:total] = grad_conv
        grad_inner = jnp.zeros((total, lanes), F32)
        for lag in range(taps):
            first = taps - 1 - lag
            grad_inner = grad_inner + taps_f[lag : lag + 1, span] * pad2[first : first + total]
        gi_ref[:, span] = grad_inner.astype(BF16)
        for lag in range(taps):
            first = 9 - taps + lag
            tap_ref[lag : lag + 1, span] = jnp.sum(
                grad_conv * pad[first : first + total, span], axis=0, keepdims=True
            )
        bias_ref[:, span] = jnp.sum(grad_conv, axis=0, keepdims=True)
    for j in range(per):
        span = slice(j * cols, (j + 1) * cols)
        value = lax.dot_general(gi_ref[...], win[0, span, :], NT, preferred_element_type=F32)
        value = value + lax.dot_general(
            gg_ref[...], win[1, span, :], NT, preferred_element_type=F32
        )
        for t in range(m):
            part[1, t * per + j] = value[t * rows : (t + 1) * rows].astype(BF16)
    to_core(1)
    to_z(0)
    to_y(1)
    finish(0)
    to_z(1)
    finish(1)

    @pl.when(swaps)
    def _():
        for p in range(2):
            swap_out(p).wait()
        out_ref[...] = res[0]
        gtok_ref[...] = res[1]

    @pl.when(jnp.logical_not(swaps))
    def _():
        out_ref[...] = fin[0]
        gtok_ref[...] = fin[1]

    for copy in sent:
        copy.wait_send()


def weight_grads(
    x_ref, g_ref, hid_ref, gi_ref, gg_ref, out_in, tok_in, tap_in, bias_in,
    din_ref, dout_ref, out_ref, tok_ref, tap_ref, bias_ref,
):
    x = x_ref[...]
    din_ref[0] = lax.dot_general(x, gi_ref[...], TN, preferred_element_type=F32)
    din_ref[1] = lax.dot_general(x, gg_ref[...], TN, preferred_element_type=F32)
    dout_ref[...] = lax.dot_general(hid_ref[...], g_ref[...], TN, preferred_element_type=F32)
    out_ref[...] = out_in[...]
    tok_ref[...] = tok_in[...]
    tap_ref[...] = tap_in[...]
    bias_ref[...] = bias_in[0]


def on_device(tokens, in_weight, conv_weight, conv_bias, out_weight, grad_out):
    n, m = lax.axis_size("dp"), lax.axis_size("seq")
    zs, ys = split_dp(n)
    rows, cols = tokens.shape
    total = rows * m
    depth = in_weight.shape[1]
    taps, chans = conv_weight.shape
    width = min(chans, 256)
    chunks = chans // width
    lanes = min(width, 128)
    vmem = pl.BlockSpec(memory_space=pltpu.VMEM)
    hbm = pl.BlockSpec(memory_space=pl.ANY)
    dma = lambda *counts: pltpu.SemaphoreType.DMA(tuple(max(i, 1) for i in counts))
    block = (rows, cols)
    shape = jax.ShapeDtypeStruct
    flops = 2 * total * depth * chans * 6
    out, gtok, x, g, hid, gi, gg, tap, bias = pl.pallas_call(
        functools.partial(body, n, m),
        out_shape=(
            shape((rows, cols), BF16), shape((rows, cols), BF16),
            shape((total, depth), BF16), shape((total, depth), BF16),
            shape((total, chans), BF16), shape((total, chans), BF16),
            shape((total, chans), BF16),
            shape((taps, chans), F32), shape((1, chans), F32),
        ),
        in_specs=[vmem, vmem, hbm, vmem, vmem, hbm],
        out_specs=(vmem,) * 9,
        scratch_shapes=[
            pltpu.VMEM(in_weight.shape, BF16),
            pltpu.VMEM(out_weight.shape, BF16),
            pltpu.VMEM((2, n) + block, BF16),
            pltpu.VMEM((m, chunks, 2, total, width), BF16),
            pltpu.VMEM((m, total, chans), BF16),
            pltpu.VMEM((2, n) + block, BF16),
            pltpu.VMEM((2, zs * ys) + block, BF16),
            pltpu.VMEM((2, max(zs * (ys - 1), 1)) + block, BF16),
            pltpu.VMEM((2, max(zs - 1, 1)) + block, BF16),
            pltpu.VMEM((2,) + block, BF16),
            pltpu.VMEM((2,) + block, BF16),
            pltpu.VMEM((total + 8, chans), F32),
            pltpu.VMEM((total + 8, lanes), F32),
            pltpu.VMEM((total, chans), F32),
            pltpu.VMEM((total, chans), F32),
            dma(2), dma(4), dma(4),
            dma(2, zs - 1), dma(2, zs * (ys - 1)), dma(2, zs * ys), dma(2, n),
            dma(chunks * (m - 1)), dma(chunks * m), dma(m - 1), dma(m),
            dma(2, zs * ys), dma(2, zs * ys),
            dma(2, zs * (ys - 1)), dma(2, zs * (ys - 1)),
            dma(2, zs - 1), dma(2, zs - 1),
        ],
        compiler_params=pltpu.CompilerParams(
            collective_id=0, has_side_effects=True, vmem_limit_bytes=56 * 2**20
        ),
        cost_estimate=pl.CostEstimate(
            flops=flops, bytes_accessed=12 * 2**20, transcendentals=2 * total * chans
        ),
        name="mixer",
    )(tokens, grad_out, in_weight, conv_weight, conv_bias.reshape(1, chans), out_weight)

    tile = min(depth, 256)
    whole = pl.BlockSpec((total, chans), lambda i: (0, 0))
    strip = pl.BlockSpec((total, tile), lambda i: (0, i))
    fixed = lambda *dims: pl.BlockSpec(dims, lambda i: (0,) * len(dims))
    token = fixed(rows, cols)
    din, dout, out, gtok, tap, bias = pl.pallas_call(
        weight_grads,
        grid=(depth // tile,),
        out_shape=(
            shape(in_weight.shape, F32), shape(out_weight.shape, F32),
            shape((rows, cols), BF16), shape((rows, cols), BF16),
            shape((taps, chans), F32), shape((chans,), F32),
        ),
        in_specs=[
            strip, strip, whole, whole, whole,
            token, token, fixed(taps, chans), fixed(1, chans),
        ],
        out_specs=(
            pl.BlockSpec((2, tile, chans), lambda i: (0, i, 0)),
            pl.BlockSpec((chans, tile), lambda i: (0, i)),
            token, token, fixed(taps, chans), fixed(chans),
        ),
        compiler_params=pltpu.CompilerParams(vmem_limit_bytes=60 * 2**20),
        name="weight_grads",
    )(x, g, hid, gi, gg, out, gtok, tap, bias)
    return (out, gtok, din, dout, tap, bias)


def solution(mesh):
    return jax.shard_map(
        on_device,
        mesh=mesh,
        in_specs=(
            P("seq", "dp"),
            P(None, "seq", "dp"),
            P(None, "dp"),
            P("dp"),
            P("dp", "seq"),
            P("seq", "dp"),
        ),
        out_specs=(
            P("seq", "dp"),
            P("seq", "dp"),
            P(None, "seq", "dp"),
            P("dp", "seq"),
            P(None, "dp"),
            P("dp"),
        ),
        check_vma=False,
    )
```

```python
import functools

import jax
import jax.numpy as jnp
from jax import lax
from jax.experimental import pallas as pl
from jax.experimental.pallas import tpu as pltpu
from jax.sharding import PartitionSpec as P

F32, BF16 = jnp.float32, jnp.bfloat16
MESH = pl.DeviceIdType.MESH
NT = (((1,), (1,)), ((), ()))


def silu_parts(value):
    sig = jax.nn.sigmoid(value)
    return (value * sig, sig * (1.0 + value * (1.0 - sig)))


def split_dp(n):
    pairs = n // 2
    ys = 2 ** ((pairs.bit_length() - 1) // 2)
    return pairs // ys, ys


def body(
    n, m, tok, gout, win_hbm, cw_ref, cb_ref, wout_hbm,
    out_ref, gtok_ref, x_ref, g_ref, hid_ref, gi_ref, gg_ref, tap_ref, bias_ref,
    win, wout, gat, slot, bslot, part, rcore, ry, rz, fin, res, pad, pad2, sa, sb,
    w_sem, sw_send, sw_recv, gz_send, gy_send, gc_send, g_recv, ex_send, ex_recv,
    bx_send, bx_recv, rc_send, rc_recv, ry_send, ry_recv, rz_send, rz_recv,
):
    zs, ys = split_dp(n)
    per = n // m
    rows, cols = tok.shape
    total = rows * m
    taps, chans = cw_ref.shape
    chunks, width = slot.shape[1], slot.shape[4]
    lanes = pad2.shape[1]
    dp, seq = lax.axis_index("dp"), lax.axis_index("seq")
    z, y, c = dp // (2 * ys), (dp // 2) % ys, dp % 2
    other = 1 - c

    def at(zz, yy, cc):
        return (zz * ys + yy) * 2 + cc

    mate = {"dp": seq * per + dp % per, "seq": dp // per}
    swaps = dp // per != seq

    def send(src, dst, ssem, rsem, where):
        return pltpu.make_async_remote_copy(
            src_ref=src, dst_ref=dst, send_sem=ssem, recv_sem=rsem,
            device_id=where, device_id_type=MESH,
        )

    loads = [
        pltpu.make_async_copy(win_hbm, win, w_sem.at[0]),
        pltpu.make_async_copy(wout_hbm, wout, w_sem.at[1]),
    ]
    for load in loads:
        load.start()

    barrier = pltpu.get_barrier_semaphore()
    near = [{"dp": at(z, y, other)}]
    near += [{"dp": at(z, (y + d) % ys, c)} for d in range(1, ys)]
    near += [{"dp": at((z + d) % zs, y, c)} for d in range(1, zs)]
    near += [{"seq": (seq + d) % m} for d in range(1, m)]
    for where in near:
        pl.semaphore_signal(barrier, inc=1, device_id=where, device_id_type=MESH)

    @pl.when(swaps)
    def _():
        pl.semaphore_signal(barrier, inc=1, device_id=mate, device_id_type=MESH)

    pl.semaphore_wait(barrier, len(near) + swaps.astype(jnp.int32))

    sent = []

    def go(*args):
        copy = send(*args)
        copy.start()
        sent.append(copy)

    def gathered(p, q, ssem, where):
        go(gat.at[p, q], gat.at[p, q], ssem, g_recv.at[p, q], where)

    def arrived(p, q):
        here = gat.at[p, q]
        send(here, here, gc_send.at[p, 0], g_recv.at[p, q], mate).wait_recv()

    sources = (tok, gout)

    def swap_in(p):
        return send(sources[p], gat.at[p, mate["dp"]], sw_send.at[p], sw_recv.at[p], mate)

    @pl.when(swaps)
    def _():
        for p in range(2):
            swap_in(p).start()
        for p in range(2):
            swap_in(p).wait_send()

    def own_block(p):
        @pl.when(swaps)
        def _():
            send(gat.at[p, dp], gat.at[p, dp], sw_send.at[p], sw_recv.at[p], mate).wait_recv()

        @pl.when(jnp.logical_not(swaps))
        def _():
            gat[p, dp] = sources[p][...]

        for d in range(1, zs):
            gathered(p, dp, gz_send.at[p, d - 1], {"dp": at((z + d) % zs, y, c)})

    def along_z(p):
        for d in range(zs):
            q = at((z + d) % zs, y, c)
            if d:
                arrived(p, q)
            for e in range(1, ys):
                i = d * (ys - 1) + e - 1
                gathered(p, q, gy_send.at[p, i], {"dp": at(z, (y + e) % ys, c)})
            gathered(p, q, gc_send.at[p, d * ys], {"dp": at(z, y, other)})

    def along_y(p, dest):
        for d in range(zs):
            for e in range(1, ys):
                q = at((z + d) % zs, (y + e) % ys, c)
                arrived(p, q)
                gathered(p, q, gc_send.at[p, d * ys + e], {"dp": at(z, y, other)})
        for d in range(zs):
            for e in range(ys):
                arrived(p, at((z + d) % zs, (y + e) % ys, other))
        for q in range(n):
            t, j = q // per, q % per
            dest[t * rows : (t + 1) * rows, j * cols : (j + 1) * cols] = gat[p, q]

    own_block(0)
    along_z(0)
    own_block(1)
    along_y(0, x_ref)
    for load in loads:
        load.wait()

    for k in range(chunks):
        span = slice(k * width, (k + 1) * width)
        for p in range(2):
            slot[seq, k, p] = jnp.dot(
                x_ref[...], win[p, :, span], preferred_element_type=F32
            ).astype(BF16)
        for d in range(1, m):
            here = slot.at[seq, k]
            go(here, here, ex_send.at[k * (m - 1) + d - 1], ex_recv.at[k * m + seq],
               {"seq": (seq + d) % m})
    along_z(1)
    along_y(1, g_ref)
    for k in range(chunks):
        span = slice(k * width, (k + 1) * width)
        bslot[seq, k] = lax.dot_general(
            g_ref[...], wout[span, :], NT, preferred_element_type=F32
        ).astype(BF16)
        for d in range(1, m):
            here = bslot.at[seq, k]
            go(here, here, bx_send.at[k * (m - 1) + d - 1], bx_recv.at[k * m + seq],
               {"seq": (seq + d) % m})

    def over_seq(read):
        value = read(0).astype(F32)
        for i in range(1, m):
            value = value + read(i).astype(F32)
        return value

    pad[0:8] = jnp.zeros((8, chans), F32)
    pad2[total : total + 8] = jnp.zeros((8, lanes), F32)
    taps_f = cw_ref[...].astype(F32)
    shift_f = cb_ref[...].astype(F32).reshape(1, chans)
    for k in range(chunks):
        for d in range(1, m):
            peer = (seq + d) % m
            here = slot.at[peer, k]
            send(here, here, ex_send.at[0], ex_recv.at[k * m + peer], mate).wait_recv()
        for col in range(0, width, lanes):
            local = slice(col, col + lanes)
            span = slice(k * width + col, k * width + col + lanes)
            inner = over_seq(lambda i: slot[i, k, 0, :, local])
            pad[8 : 8 + total, span] = inner.astype(BF16).astype(F32)
            gate_in = over_seq(lambda i: slot[i, k, 1, :, local])
            gate, gate_slope = silu_parts(gate_in.astype(BF16).astype(F32))
            conv = jnp.broadcast_to(shift_f[:, span], (total, lanes))
            for lag in range(taps):
                first = 9 - taps + lag
                conv = conv + taps_f[lag : lag + 1, span] * pad[first : first + total, span]
            act, act_slope = silu_parts(conv)
            hid_ref[:, span] = (act * gate).astype(BF16)
            sa[:, span] = gate * act_slope
            sb[:, span] = act * gate_slope

    def core_copy(p, d, e, which):
        zz, yy = (z + d) % zs, (y + e) % ys
        i = zz * ys + yy
        return send(part.at[p, at(zz, yy, which)], rcore.at[p, i], rc_send.at[p, i],
                    rc_recv.at[p, i], {"dp": at(z, y, other)})

    def to_core(p):
        for e in range(ys - 1, -1, -1):
            for d in range(zs - 1, -1, -1):
                copy = core_copy(p, d, e, other)
                copy.start()
                sent.append(copy)

    def to_y(p):
        for e in range(ys - 1, 0, -1):
            for d in range(zs - 1, -1, -1):
                zz, yy = (z + d) % zs, (y + e) % ys
                core_copy(p, d, e, other).wait_recv()
                q = at(zz, yy, c)
                value = part[p, q].astype(F32) + rcore[p, zz * ys + yy].astype(F32)
                part[p, q] = value.astype(BF16)
                i = (e - 1) * zs + zz
                go(part.at[p, q], ry.at[p, i], ry_send.at[p, i], ry_recv.at[p, i],
                   {"dp": at(z, yy, c)})

    def to_z(p):
        for d in range(zs - 1, -1, -1):
            zz = (z + d) % zs
            core_copy(p, d, 0, other).wait_recv()
            q = at(zz, y, c)
            value = part[p, q].astype(F32) + rcore[p, zz * ys + y].astype(F32)
            for e in range(1, ys):
                i = (e - 1) * zs + zz
                send(part.at[p, q], ry.at[p, i], ry_send.at[p, i], ry_recv.at[p, i],
                     mate).wait_recv()
                value = value + ry[p, i].astype(F32)
            if d:
                part[p, q] = value.astype(BF16)
                go(part.at[p, q], rz.at[p, d - 1], rz_send.at[p, d - 1], rz_recv.at[p, d - 1],
                   {"dp": at(zz, y, c)})
            else:
                part[p, q] = value.astype(BF16)

    def swap_out(p):
        return send(fin.at[p], res.at[p], sw_send.at[2 + p], sw_recv.at[2 + p], mate)

    def finish(p):
        value = part[p, dp].astype(F32)
        for i in range(zs - 1):
            send(part.at[p, dp], rz.at[p, i], rz_send.at[p, i], rz_recv.at[p, i],
                 mate).wait_recv()
            value = value + rz[p, i].astype(F32)
        fin[p] = value.astype(BF16)

        @pl.when(swaps)
        def _():
            swap_out(p).start()

    for j in range(per):
        span = slice(j * cols, (j + 1) * cols)
        value = jnp.dot(hid_ref[...], wout[:, span], preferred_element_type=F32)
        for t in range(m):
            part[0, t * per + j] = value[t * rows : (t + 1) * rows].astype(BF16)
    to_core(0)
    to_y(0)

    for col in range(0, chans, lanes):
        span = slice(col, col + lanes)
        k, local = col // width, slice(col % width, col % width + lanes)
        if col % width == 0:
            for d in range(1, m):
                peer = (seq + d) % m
                here = bslot.at[peer, k]
                send(here, here, bx_send.at[0], bx_recv.at[k * m + peer], mate).wait_recv()
        back = over_seq(lambda i: bslot[i, k, :, local])
        gg_ref[:, span] = (back * sb[:, span]).astype(BF16)
        grad_conv = (back * sa[:, span]).astype(BF16).astype(F32)
        pad2[0:total] = grad_conv
        grad_inner = jnp.zeros((total, lanes), F32)
        for lag in range(taps):
            first = taps - 1 - lag
            grad_inner = grad_inner + taps_f[lag : lag + 1, span] * pad2[first : first + total]
        gi_ref[:, span] = grad_inner.astype(BF16)
        for lag in range(taps):
            first = 9 - taps + lag
            tap_ref[lag : lag + 1, span] = jnp.sum(
                grad_conv * pad[first : first + total, span], axis=0, keepdims=True
            )
        bias_ref[:, span] = jnp.sum(grad_conv, axis=0, keepdims=True)
    for j in range(per):
        span = slice(j * cols, (j + 1) * cols)
        value = lax.dot_general(gi_ref[...], win[0, span, :], NT, preferred_element_type=F32)
        value = value + lax.dot_general(
            gg_ref[...], win[1, span, :], NT, preferred_element_type=F32
        )
        for t in range(m):
            part[1, t * per + j] = value[t * rows : (t + 1) * rows].astype(BF16)
    to_core(1)
    to_z(0)
    to_y(1)
    finish(0)
    to_z(1)
    finish(1)

    @pl.when(swaps)
    def _():
        for p in range(2):
            swap_out(p).wait()
        out_ref[...] = res[0]
        gtok_ref[...] = res[1]

    @pl.when(jnp.logical_not(swaps))
    def _():
        out_ref[...] = fin[0]
        gtok_ref[...] = fin[1]

    for copy in sent:
        copy.wait_send()


def weight_grads(
    x_ref, g_ref, hid_ref, gi_ref, gg_ref, out_in, tok_in, tap_in, bias_in,
    din_ref, dout_ref, out_ref, tok_ref, tap_ref, bias_ref, turned,
):
    @pl.when(pl.program_id(0) == 0)
    def _():
        turned[...] = hid_ref[...].T
        out_ref[...] = out_in[...]
        tok_ref[...] = tok_in[...]
        tap_ref[...] = tap_in[...]
        bias_ref[...] = bias_in[0]

    x = x_ref[...].T
    din_ref[0] = jnp.dot(x, gi_ref[...], preferred_element_type=F32)
    din_ref[1] = jnp.dot(x, gg_ref[...], preferred_element_type=F32)
    dout_ref[...] = jnp.dot(turned[...], g_ref[...], preferred_element_type=F32)


def on_device(tokens, in_weight, conv_weight, conv_bias, out_weight, grad_out):
    n, m = lax.axis_size("dp"), lax.axis_size("seq")
    zs, ys = split_dp(n)
    rows, cols = tokens.shape
    total = rows * m
    depth = in_weight.shape[1]
    taps, chans = conv_weight.shape
    width = min(chans, 256)
    chunks = chans // width
    lanes = min(width, 128)
    vmem = pl.BlockSpec(memory_space=pltpu.VMEM)
    hbm = pl.BlockSpec(memory_space=pl.ANY)
    dma = lambda *counts: pltpu.SemaphoreType.DMA(tuple(max(i, 1) for i in counts))
    block = (rows, cols)
    shape = jax.ShapeDtypeStruct
    flops = 2 * total * depth * chans * 6
    out, gtok, x, g, hid, gi, gg, tap, bias = pl.pallas_call(
        functools.partial(body, n, m),
        out_shape=(
            shape((rows, cols), BF16), shape((rows, cols), BF16),
            shape((total, depth), BF16), shape((total, depth), BF16),
            shape((total, chans), BF16), shape((total, chans), BF16),
            shape((total, chans), BF16),
            shape((taps, chans), F32), shape((1, chans), F32),
        ),
        in_specs=[vmem, vmem, hbm, vmem, vmem, hbm],
        out_specs=(vmem,) * 9,
        scratch_shapes=[
            pltpu.VMEM(in_weight.shape, BF16),
            pltpu.VMEM(out_weight.shape, BF16),
            pltpu.VMEM((2, n) + block, BF16),
            pltpu.VMEM((m, chunks, 2, total, width), BF16),
            pltpu.VMEM((m, chunks, total, width), BF16),
            pltpu.VMEM((2, n) + block, BF16),
            pltpu.VMEM((2, zs * ys) + block, BF16),
            pltpu.VMEM((2, max(zs * (ys - 1), 1)) + block, BF16),
            pltpu.VMEM((2, max(zs - 1, 1)) + block, BF16),
            pltpu.VMEM((2,) + block, BF16),
            pltpu.VMEM((2,) + block, BF16),
            pltpu.VMEM((total + 8, chans), F32),
            pltpu.VMEM((total + 8, lanes), F32),
            pltpu.VMEM((total, chans), F32),
            pltpu.VMEM((total, chans), F32),
            dma(2), dma(4), dma(4),
            dma(2, zs - 1), dma(2, zs * (ys - 1)), dma(2, zs * ys), dma(2, n),
            dma(chunks * (m - 1)), dma(chunks * m), dma(chunks * (m - 1)), dma(chunks * m),
            dma(2, zs * ys), dma(2, zs * ys),
            dma(2, zs * (ys - 1)), dma(2, zs * (ys - 1)),
            dma(2, zs - 1), dma(2, zs - 1),
        ],
        compiler_params=pltpu.CompilerParams(
            collective_id=0, has_side_effects=True, vmem_limit_bytes=56 * 2**20
        ),
        cost_estimate=pl.CostEstimate(
            flops=flops, bytes_accessed=12 * 2**20, transcendentals=2 * total * chans
        ),
        name="mixer",
    )(tokens, grad_out, in_weight, conv_weight, conv_bias, out_weight)

    tile = min(depth, 256)
    whole = pl.BlockSpec((total, chans), lambda i: (0, 0))
    strip = pl.BlockSpec((total, tile), lambda i: (0, i))
    fixed = lambda *dims: pl.BlockSpec(dims, lambda i: (0,) * len(dims))
    token = fixed(rows, cols)
    din, dout, out, gtok, tap, bias = pl.pallas_call(
        weight_grads,
        grid=(depth // tile,),
        out_shape=(
            shape(in_weight.shape, F32), shape(out_weight.shape, F32),
            shape((rows, cols), BF16), shape((rows, cols), BF16),
            shape((taps, chans), F32), shape((chans,), F32),
        ),
        in_specs=[
            strip, strip, whole, whole, whole,
            token, token, fixed(taps, chans), fixed(1, chans),
        ],
        out_specs=(
            pl.BlockSpec((2, tile, chans), lambda i: (0, i, 0)),
            pl.BlockSpec((chans, tile), lambda i: (0, i)),
            token, token, fixed(taps, chans), fixed(chans),
        ),
        scratch_shapes=[pltpu.VMEM((chans, total), BF16)],
        compiler_params=pltpu.CompilerParams(vmem_limit_bytes=60 * 2**20),
        name="weight_grads",
    )(x, g, hid, gi, gg, out, gtok, tap, bias)
    return (out, gtok, din, dout, tap, bias)


def solution(mesh):
    return jax.shard_map(
        on_device,
        mesh=mesh,
        in_specs=(
            P("seq", "dp"),
            P(None, "seq", "dp"),
            P(None, "dp"),
            P("dp"),
            P("dp", "seq"),
            P("seq", "dp"),
        ),
        out_specs=(
            P("seq", "dp"),
            P("seq", "dp"),
            P(None, "seq", "dp"),
            P("dp", "seq"),
            P(None, "dp"),
            P("dp"),
        ),
        check_vma=False,
    )
```

```python
import functools

import jax
import jax.numpy as jnp
from jax import lax
from jax.experimental import pallas as pl
from jax.experimental.pallas import tpu as pltpu
from jax.sharding import PartitionSpec as P

F32, BF16 = jnp.float32, jnp.bfloat16
MESH = pl.DeviceIdType.MESH
NT = (((1,), (1,)), ((), ()))


def silu_parts(value):
    sig = jax.nn.sigmoid(value)
    return (value * sig, sig * (1.0 + value * (1.0 - sig)))


def split_dp(n):
    pairs = n // 2
    ys = 2 ** ((pairs.bit_length() - 1) // 2)
    return pairs // ys, ys


def body(
    n, m, tok, gout, win_hbm, cw_ref, cb_ref, wout_hbm,
    out_ref, gtok_ref, x_ref, g_ref, hid_ref, gi_ref, gg_ref, tap_ref, bias_ref,
    win, wout, gat, slot, bslot, part, rcore, ry, rz, fin, res, pad, pad2, sa, sb,
    w_sem, sw_send, sw_recv, gz_send, gy_send, gc_send, g_recv, ex_send, ex_recv,
    bx_send, bx_recv, rc_send, rc_recv, ry_send, ry_recv, rz_send, rz_recv,
):
    zs, ys = split_dp(n)
    per = n // m
    rows, cols = tok.shape
    total = rows * m
    taps, chans = cw_ref.shape
    chunks, width = slot.shape[1], slot.shape[4]
    lanes = pad2.shape[1]
    dp, seq = lax.axis_index("dp"), lax.axis_index("seq")
    z, y, c = dp // (2 * ys), (dp // 2) % ys, dp % 2
    other = 1 - c

    def at(zz, yy, cc):
        return (zz * ys + yy) * 2 + cc

    mate = {"dp": seq * per + dp % per, "seq": dp // per}
    swaps = dp // per != seq

    def send(src, dst, ssem, rsem, where):
        return pltpu.make_async_remote_copy(
            src_ref=src, dst_ref=dst, send_sem=ssem, recv_sem=rsem,
            device_id=where, device_id_type=MESH,
        )

    loads = [
        pltpu.make_async_copy(win_hbm, win, w_sem.at[0]),
        pltpu.make_async_copy(wout_hbm, wout, w_sem.at[1]),
    ]
    for load in loads:
        load.start()

    barrier = pltpu.get_barrier_semaphore()
    near = [{"dp": at(z, y, other)}]
    near += [{"dp": at(z, (y + d) % ys, c)} for d in range(1, ys)]
    near += [{"dp": at((z + d) % zs, y, c)} for d in range(1, zs)]
    near += [{"seq": (seq + d) % m} for d in range(1, m)]
    for where in near:
        pl.semaphore_signal(barrier, inc=1, device_id=where, device_id_type=MESH)

    @pl.when(swaps)
    def _():
        pl.semaphore_signal(barrier, inc=1, device_id=mate, device_id_type=MESH)

    pl.semaphore_wait(barrier, len(near) + swaps.astype(jnp.int32))

    sent = []

    def go(*args):
        copy = send(*args)
        copy.start()
        sent.append(copy)

    def gathered(p, q, ssem, where):
        go(gat.at[p, q], gat.at[p, q], ssem, g_recv.at[p, q], where)

    def arrived(p, q):
        here = gat.at[p, q]
        send(here, here, gc_send.at[p, 0], g_recv.at[p, q], mate).wait_recv()

    sources = (tok, gout)

    def swap_in(p):
        return send(sources[p], gat.at[p, mate["dp"]], sw_send.at[p], sw_recv.at[p], mate)

    @pl.when(swaps)
    def _():
        for p in range(2):
            swap_in(p).start()
        for p in range(2):
            swap_in(p).wait_send()

    def own_block(p):
        @pl.when(swaps)
        def _():
            send(gat.at[p, dp], gat.at[p, dp], sw_send.at[p], sw_recv.at[p], mate).wait_recv()

        @pl.when(jnp.logical_not(swaps))
        def _():
            gat[p, dp] = sources[p][...]

        for d in range(1, zs):
            gathered(p, dp, gz_send.at[p, d - 1], {"dp": at((z + d) % zs, y, c)})

    def along_z(p):
        for d in range(zs):
            q = at((z + d) % zs, y, c)
            if d:
                arrived(p, q)
            for e in range(1, ys):
                i = d * (ys - 1) + e - 1
                gathered(p, q, gy_send.at[p, i], {"dp": at(z, (y + e) % ys, c)})
            gathered(p, q, gc_send.at[p, d * ys], {"dp": at(z, y, other)})

    def along_y(p, dest):
        for d in range(zs):
            for e in range(1, ys):
                q = at((z + d) % zs, (y + e) % ys, c)
                arrived(p, q)
                gathered(p, q, gc_send.at[p, d * ys + e], {"dp": at(z, y, other)})
        for d in range(zs):
            for e in range(ys):
                arrived(p, at((z + d) % zs, (y + e) % ys, other))
        for q in range(n):
            t, j = q // per, q % per
            dest[t * rows : (t + 1) * rows, j * cols : (j + 1) * cols] = gat[p, q]

    own_block(0)
    along_z(0)
    own_block(1)
    along_y(0, x_ref)
    for load in loads:
        load.wait()

    for k in range(chunks):
        span = slice(k * width, (k + 1) * width)
        for p in range(2):
            slot[seq, k, p] = jnp.dot(
                x_ref[...], win[p, :, span], preferred_element_type=F32
            ).astype(BF16)
        for d in range(1, m):
            here = slot.at[seq, k]
            go(here, here, ex_send.at[k * (m - 1) + d - 1], ex_recv.at[k * m + seq],
               {"seq": (seq + d) % m})
    along_z(1)
    along_y(1, g_ref)
    for k in range(chunks):
        span = slice(k * width, (k + 1) * width)
        bslot[seq, k] = lax.dot_general(
            g_ref[...], wout[span, :], NT, preferred_element_type=F32
        ).astype(BF16)
        for d in range(1, m):
            here = bslot.at[seq, k]
            go(here, here, bx_send.at[k * (m - 1) + d - 1], bx_recv.at[k * m + seq],
               {"seq": (seq + d) % m})

    def over_seq(read):
        value = read(0).astype(F32)
        for i in range(1, m):
            value = value + read(i).astype(F32)
        return value

    pad[0:8] = jnp.zeros((8, chans), F32)
    pad2[total : total + 8] = jnp.zeros((8, lanes), F32)
    taps_f = cw_ref[...].astype(F32)
    shift_f = cb_ref[...].astype(F32).reshape(1, chans)
    for k in range(chunks):
        for d in range(1, m):
            peer = (seq + d) % m
            here = slot.at[peer, k]
            send(here, here, ex_send.at[0], ex_recv.at[k * m + peer], mate).wait_recv()
        for col in range(0, width, lanes):
            local = slice(col, col + lanes)
            span = slice(k * width + col, k * width + col + lanes)
            inner = over_seq(lambda i: slot[i, k, 0, :, local])
            pad[8 : 8 + total, span] = inner.astype(BF16).astype(F32)
            gate_in = over_seq(lambda i: slot[i, k, 1, :, local])
            gate, gate_slope = silu_parts(gate_in.astype(BF16).astype(F32))
            conv = jnp.broadcast_to(shift_f[:, span], (total, lanes))
            for lag in range(taps):
                first = 9 - taps + lag
                conv = conv + taps_f[lag : lag + 1, span] * pad[first : first + total, span]
            act, act_slope = silu_parts(conv)
            hid_ref[:, span] = (act * gate).astype(BF16)
            sa[:, span] = gate * act_slope
            sb[:, span] = act * gate_slope

    def core_copy(p, d, e, which):
        zz, yy = (z + d) % zs, (y + e) % ys
        i = zz * ys + yy
        return send(part.at[p, at(zz, yy, which)], rcore.at[p, i], rc_send.at[p, i],
                    rc_recv.at[p, i], {"dp": at(z, y, other)})

    def to_core(p):
        for e in range(ys - 1, -1, -1):
            for d in range(zs - 1, -1, -1):
                copy = core_copy(p, d, e, other)
                copy.start()
                sent.append(copy)

    def to_y(p):
        for e in range(ys - 1, 0, -1):
            for d in range(zs - 1, -1, -1):
                zz, yy = (z + d) % zs, (y + e) % ys
                core_copy(p, d, e, other).wait_recv()
                q = at(zz, yy, c)
                value = part[p, q].astype(F32) + rcore[p, zz * ys + yy].astype(F32)
                part[p, q] = value.astype(BF16)
                i = (e - 1) * zs + zz
                go(part.at[p, q], ry.at[p, i], ry_send.at[p, i], ry_recv.at[p, i],
                   {"dp": at(z, yy, c)})

    def to_z(p):
        for d in range(zs - 1, -1, -1):
            zz = (z + d) % zs
            core_copy(p, d, 0, other).wait_recv()
            q = at(zz, y, c)
            value = part[p, q].astype(F32) + rcore[p, zz * ys + y].astype(F32)
            for e in range(1, ys):
                i = (e - 1) * zs + zz
                send(part.at[p, q], ry.at[p, i], ry_send.at[p, i], ry_recv.at[p, i],
                     mate).wait_recv()
                value = value + ry[p, i].astype(F32)
            if d:
                part[p, q] = value.astype(BF16)
                go(part.at[p, q], rz.at[p, d - 1], rz_send.at[p, d - 1], rz_recv.at[p, d - 1],
                   {"dp": at(zz, y, c)})
            else:
                part[p, q] = value.astype(BF16)

    def swap_out(p):
        return send(fin.at[p], res.at[p], sw_send.at[2 + p], sw_recv.at[2 + p], mate)

    def finish(p):
        value = part[p, dp].astype(F32)
        for i in range(zs - 1):
            send(part.at[p, dp], rz.at[p, i], rz_send.at[p, i], rz_recv.at[p, i],
                 mate).wait_recv()
            value = value + rz[p, i].astype(F32)
        fin[p] = value.astype(BF16)

        @pl.when(swaps)
        def _():
            swap_out(p).start()

    for j in range(per):
        span = slice(j * cols, (j + 1) * cols)
        value = jnp.dot(hid_ref[...], wout[:, span], preferred_element_type=F32)
        for t in range(m):
            part[0, t * per + j] = value[t * rows : (t + 1) * rows].astype(BF16)
    to_core(0)
    to_y(0)

    for col in range(0, chans, lanes):
        span = slice(col, col + lanes)
        k, local = col // width, slice(col % width, col % width + lanes)
        if col % width == 0:
            for d in range(1, m):
                peer = (seq + d) % m
                here = bslot.at[peer, k]
                send(here, here, bx_send.at[0], bx_recv.at[k * m + peer], mate).wait_recv()
        back = over_seq(lambda i: bslot[i, k, :, local])
        gg_ref[:, span] = (back * sb[:, span]).astype(BF16)
        grad_conv = (back * sa[:, span]).astype(BF16).astype(F32)
        pad2[0:total] = grad_conv
        grad_inner = jnp.zeros((total, lanes), F32)
        for lag in range(taps):
            first = taps - 1 - lag
            grad_inner = grad_inner + taps_f[lag : lag + 1, span] * pad2[first : first + total]
        gi_ref[:, span] = grad_inner.astype(BF16)
        for lag in range(taps):
            first = 9 - taps + lag
            tap_ref[lag : lag + 1, span] = jnp.sum(
                grad_conv * pad[first : first + total, span], axis=0, keepdims=True
            )
        bias_ref[:, span] = jnp.sum(grad_conv, axis=0, keepdims=True)
    for j in range(per):
        span = slice(j * cols, (j + 1) * cols)
        value = lax.dot_general(gi_ref[...], win[0, span, :], NT, preferred_element_type=F32)
        value = value + lax.dot_general(
            gg_ref[...], win[1, span, :], NT, preferred_element_type=F32
        )
        for t in range(m):
            part[1, t * per + j] = value[t * rows : (t + 1) * rows].astype(BF16)
    to_core(1)
    to_z(0)
    to_y(1)
    finish(0)
    to_z(1)
    finish(1)

    @pl.when(swaps)
    def _():
        for p in range(2):
            swap_out(p).wait()
        out_ref[...] = res[0]
        gtok_ref[...] = res[1]

    @pl.when(jnp.logical_not(swaps))
    def _():
        out_ref[...] = fin[0]
        gtok_ref[...] = fin[1]

    for copy in sent:
        copy.wait_send()


def weight_grads(
    x_ref, g_ref, hid_ref, gi_ref, gg_ref, out_in, tok_in, tap_in, bias_in,
    din_ref, dout_ref, out_ref, tok_ref, tap_ref, bias_ref, turned,
):
    @pl.when(pl.program_id(0) == 0)
    def _():
        turned[...] = hid_ref[...].T
        out_ref[...] = out_in[...]
        tok_ref[...] = tok_in[...]
        tap_ref[...] = tap_in[...]
        bias_ref[...] = bias_in[0]

    x = x_ref[...].T
    din_ref[0] = jnp.dot(x, gi_ref[...], preferred_element_type=F32)
    din_ref[1] = jnp.dot(x, gg_ref[...], preferred_element_type=F32)
    dout_ref[...] = jnp.dot(turned[...], g_ref[...], preferred_element_type=F32)


def on_device(tokens, in_weight, conv_weight, conv_bias, out_weight, grad_out):
    n, m = lax.axis_size("dp"), lax.axis_size("seq")
    zs, ys = split_dp(n)
    rows, cols = tokens.shape
    total = rows * m
    depth = in_weight.shape[1]
    taps, chans = conv_weight.shape
    width = min(chans, 256)
    chunks = chans // width
    lanes = min(width, 128)
    vmem = pl.BlockSpec(memory_space=pltpu.VMEM)
    hbm = pl.BlockSpec(memory_space=pl.ANY)
    dma = lambda *counts: pltpu.SemaphoreType.DMA(tuple(max(i, 1) for i in counts))
    block = (rows, cols)
    shape = jax.ShapeDtypeStruct
    flops = 2 * total * depth * chans * 6
    out, gtok, x, g, hid, gi, gg, tap, bias = pl.pallas_call(
        functools.partial(body, n, m),
        out_shape=(
            shape((rows, cols), BF16), shape((rows, cols), BF16),
            shape((total, depth), BF16), shape((total, depth), BF16),
            shape((total, chans), BF16), shape((total, chans), BF16),
            shape((total, chans), BF16),
            shape((taps, chans), F32), shape((1, chans), F32),
        ),
        in_specs=[vmem, vmem, hbm, vmem, vmem, hbm],
        out_specs=(vmem,) * 9,
        scratch_shapes=[
            pltpu.VMEM(in_weight.shape, BF16),
            pltpu.VMEM(out_weight.shape, BF16),
            pltpu.VMEM((2, n) + block, BF16),
            pltpu.VMEM((m, chunks, 2, total, width), BF16),
            pltpu.VMEM((m, chunks, total, width), BF16),
            pltpu.VMEM((2, n) + block, BF16),
            pltpu.VMEM((2, zs * ys) + block, BF16),
            pltpu.VMEM((2, max(zs * (ys - 1), 1)) + block, BF16),
            pltpu.VMEM((2, max(zs - 1, 1)) + block, BF16),
            pltpu.VMEM((2,) + block, BF16),
            pltpu.VMEM((2,) + block, BF16),
            pltpu.VMEM((total + 8, chans), F32),
            pltpu.VMEM((total + 8, lanes), F32),
            pltpu.VMEM((total, chans), F32),
            pltpu.VMEM((total, chans), F32),
            dma(2), dma(4), dma(4),
            dma(2, zs - 1), dma(2, zs * (ys - 1)), dma(2, zs * ys), dma(2, n),
            dma(chunks * (m - 1)), dma(chunks * m), dma(chunks * (m - 1)), dma(chunks * m),
            dma(2, zs * ys), dma(2, zs * ys),
            dma(2, zs * (ys - 1)), dma(2, zs * (ys - 1)),
            dma(2, zs - 1), dma(2, zs - 1),
        ],
        compiler_params=pltpu.CompilerParams(
            collective_id=0, has_side_effects=True, vmem_limit_bytes=56 * 2**20
        ),
        cost_estimate=pl.CostEstimate(
            flops=flops, bytes_accessed=12 * 2**20, transcendentals=2 * total * chans
        ),
        name="mixer",
    )(tokens, grad_out, in_weight, conv_weight, conv_bias, out_weight)

    tile = min(depth, 512)
    whole = pl.BlockSpec((total, chans), lambda i: (0, 0))
    strip = pl.BlockSpec((total, tile), lambda i: (0, i))
    fixed = lambda *dims: pl.BlockSpec(dims, lambda i: (0,) * len(dims))
    token = fixed(rows, cols)
    din, dout, out, gtok, tap, bias = pl.pallas_call(
        weight_grads,
        grid=(depth // tile,),
        out_shape=(
            shape(in_weight.shape, F32), shape(out_weight.shape, F32),
            shape((rows, cols), BF16), shape((rows, cols), BF16),
            shape((taps, chans), F32), shape((chans,), F32),
        ),
        in_specs=[
            strip, strip, whole, whole, whole,
            token, token, fixed(taps, chans), fixed(1, chans),
        ],
        out_specs=(
            pl.BlockSpec((2, tile, chans), lambda i: (0, i, 0)),
            pl.BlockSpec((chans, tile), lambda i: (0, i)),
            token, token, fixed(taps, chans), fixed(chans),
        ),
        scratch_shapes=[pltpu.VMEM((chans, total), BF16)],
        compiler_params=pltpu.CompilerParams(vmem_limit_bytes=60 * 2**20),
        name="weight_grads",
    )(x, g, hid, gi, gg, out, gtok, tap, bias)
    return (out, gtok, din, dout, tap, bias)


def solution(mesh):
    return jax.shard_map(
        on_device,
        mesh=mesh,
        in_specs=(
            P("seq", "dp"),
            P(None, "seq", "dp"),
            P(None, "dp"),
            P("dp"),
            P("dp", "seq"),
            P("seq", "dp"),
        ),
        out_specs=(
            P("seq", "dp"),
            P("seq", "dp"),
            P(None, "seq", "dp"),
            P("dp", "seq"),
            P(None, "dp"),
            P("dp"),
        ),
        check_vma=False,
    )
```
